512 devices in a mesh: grp: 8 (over y, core), dev: 64 (over x, z).
Axes of the slice: x: 4, y: 4, z: 16, core: 2. Of those that a mesh axis runs over, the one named last changes fastest.
Arguments:
- embeddings: bfloat16 [196608, 4096], P(('grp', 'dev')), may hold values from -256 to 256
- sketch_matrix: bfloat16 [4096, 128], P('dev'), may hold values from -0.09375 to 0.09375
Outputs:
- orthobasis: float32 [196608, 128], P(('grp', 'dev'))
- projected: float32 [4096, 128], P('dev')
The draws below stay inside these ranges and needn't reach their ends.
All inputs are finite; a program needn't handle non-finite values.
Results may differ from the reference program's by a relative error of at most 0.0065.
Values may be sent and summed in bfloat16 or wider, within the bound.
A program may use at most 64 MiB of HBM per device.

```python
import jax
import jax.numpy as jnp
from jax import lax

D = 4096
K = 128
ROWS_DEV = 384
ROWS = 196608


def draw_embeddings(key, part):
    key = jax.random.fold_in(key, 7)
    base_key, scale_key, spike_key = jax.random.split(key, 3)
    blocks = ROWS // ROWS_DEV
    values = jnp.clip(jax.random.normal(base_key, (ROWS, D), jnp.float32), -5.0, 5.0)
    block_of = jnp.arange(ROWS, dtype=jnp.int32) // ROWS_DEV
    ramp_scale = 0.7 * 2.0 ** (block_of.astype(jnp.float32) / max(blocks - 1, 1))
    jitter = jax.random.uniform(scale_key, (ROWS,), jnp.float32, 0.85, 1.15)
    spike_order = jax.random.permutation(spike_key, blocks).astype(jnp.int32)
    span_cols = D // blocks
    target = spike_order[block_of]
    column_block = jnp.arange(D, dtype=jnp.int32) // span_cols
    spike_gain = jnp.where(column_block[None, :] == target[:, None], 20.0, 1.0)
    row_scale = ramp_scale * jitter
    return (values * spike_gain * row_scale[:, None]).astype(jnp.bfloat16)


def shard_levels(rng, dims, cuts, low, largest):
    def one(dim, blocks):
        heights = jax.random.uniform(jax.random.fold_in(jax.random.fold_in(rng, 6), dim), (blocks,), jnp.float32, low / len(cuts), largest / len(cuts))
        return jnp.repeat(jnp.exp(heights), dims[dim] // blocks).reshape((-1,) + (1,) * (len(dims) - dim - 1))

    factor_of = one(*cuts[0])
    for cut in cuts[1:]:
        factor_of = factor_of * one(*cut)
    return factor_of


def centred(own_key, dims, scale, reach, shards=(), kind=jnp.bfloat16):
    values = jax.random.normal(own_key, dims, jnp.float32) * scale
    if len(shards) > 0:
        values = shard_levels(own_key, dims, shards, -0.22, 0.18) * values
    return jnp.clip(values, min=-reach, max=reach).astype(kind)


def setup_inputs(seed: int = 0) -> dict:
    arg_keys = jax.random.split(jax.random.key(seed), 3)
    return {
        "embeddings": draw_embeddings(jax.random.fold_in(arg_keys[2], 71), 0),
        "sketch_matrix": centred(arg_keys[1], (D, K), D ** -0.5, 0.09375, ((0, 64),)),
    }


def contract_rows(left, right):
    return lax.dot_general(left.astype(jnp.float32), right.astype(jnp.float32), (((0,), (0,)), ((), ())), preferred_element_type=jnp.float32)

def reference(embeddings, sketch_matrix):
    sketched = jnp.dot(embeddings.astype(jnp.float32), sketch_matrix.astype(jnp.float32), preferred_element_type=jnp.float32).astype(jnp.bfloat16)
    powered = (contract_rows(embeddings, sketched) / ROWS).astype(jnp.bfloat16)
    refined = jnp.dot(embeddings.astype(jnp.float32), powered.astype(jnp.float32), preferred_element_type=jnp.float32)
    gram = jnp.dot(refined.T, refined, precision=lax.Precision.HIGHEST) / ROWS
    triangle = jnp.linalg.cholesky(gram)
    orthobasis = jax.scipy.linalg.solve_triangular(triangle, refined.T, lower=True).T
    basis_half = orthobasis.astype(jnp.bfloat16)
    projected = contract_rows(embeddings, basis_half) * (D ** 0.5 / ROWS)
    return (orthobasis, projected)
```

```python
import jax
import jax.numpy as jnp
from jax import lax
from jax.experimental import pallas as pl
from jax.experimental.pallas import tpu as pltpu
from jax.sharding import PartitionSpec as P

X, Y, Z, C = 4, 4, 16, 2
XY = X * Y
ZL = Z // C
DEVICES = XY * Z * C
PIECE = 16
CHUNK = ZL * Y * PIECE
PANEL = 16
HIGHEST = lax.Precision.HIGHEST
F32, BF16 = jnp.float32, jnp.bfloat16


def nt(a, b, precision=None):
    return lax.dot_general(
        a, b, (((1,), (1,)), ((), ())), precision=precision, preferred_element_type=F32
    )


def tn(a, b, precision=None):
    return lax.dot_general(
        a, b, (((0,), (0,)), ((), ())), precision=precision, preferred_element_type=F32
    )


def nn(a, b, precision=None):
    return jnp.dot(a, b, precision=precision, preferred_element_type=F32)


def inverse_factor_steps(gram):
    k = gram.shape[0]
    rows = lax.broadcasted_iota(jnp.int32, (PANEL, 1), 0)
    eye = (
        lax.broadcasted_iota(jnp.int32, (k, k), 0) == lax.broadcasted_iota(jnp.int32, (k, k), 1)
    ).astype(F32)
    trailing = jnp.concatenate([gram, eye], axis=1)
    done = []
    for base in range(0, k, PANEL):
        panel = trailing[:PANEL]
        cols = [
            jnp.broadcast_to(panel[:, base + t : base + t + 1], (PANEL, k)) for t in range(PANEL)
        ]
        left, right = panel[:, :k], panel[:, k:]
        for j in range(PANEL):
            pivot = lax.rsqrt(cols[j][j : j + 1])
            factor = cols[j] * pivot
            below = jnp.where(rows > j, factor, 0.0)
            for t in range(j + 1, PANEL):
                cols[t] = cols[t] - below * factor[t : t + 1]
            scale = jnp.where(rows == j, pivot, 1.0)
            left_row, right_row = left[j : j + 1] * pivot, right[j : j + 1] * pivot
            left = left * scale - below * left_row
            right = right * scale - below * right_row
        done.append(right)
        if base + PANEL < k:
            both = jnp.concatenate([left, right], axis=1)
            trailing = trailing[PANEL:] - tn(left[:, base + PANEL :], both, HIGHEST)
            yield None
    yield jnp.concatenate(done, axis=0)


def kernel(
    e_hbm, s_ref, ortho_ref, proj_ref,
    e_ref, s_full, p_full, part_a, part_b, core_a, core_b, sum_a, sum_b, xy_a, xy_b,
    zout_a, zout_b, z_a, z_b, gpart, g1, g2, gfull, yfin,
    load_sem,
    ags_z_s, ags_z_r, ags_x_s, ags_x_r, ags_c_s, ags_c_r,
    agp_z_s, agp_z_r, agp_x_s, agp_x_r, agp_c_s, agp_c_r,
    rsa_c_s, rsa_c_r, rsa_x_s, rsa_x_r, rsa_z_s, rsa_z_r,
    rsb_c_s, rsb_c_r, rsb_x_s, rsb_x_r, rsb_z_s, rsb_z_r,
    g1_s, g1_r, g2_s, g2_r, g3_s, g3_r, f_s, f_r,
):
    grp, dev = lax.axis_index("grp"), lax.axis_index("dev")
    y, c = grp // C, grp % C
    x, z = dev // Z, dev % Z
    other = 1 - c
    half, zl = z // ZL, z % ZL
    owner = c == half
    rows_all = DEVICES * e_ref.shape[0]

    def at(x_, y_, z_, c_):
        return (y_ * C + c_, x_ * Z + z_)

    def xy(k):
        kx, ky = k // Y, k % Y
        return ((x + kx) % X, (y + ky) % Y), ((x + X - kx) % X, (y + Y - ky) % Y)

    drains = []

    def send(src, dst, ssem, rsem, to, when=None):
        copy = pltpu.make_async_remote_copy(
            src_ref=src, dst_ref=dst, send_sem=ssem, recv_sem=rsem,
            device_id=to, device_id_type=pl.DeviceIdType.MESH,
        )

        def start():
            copy.start()

        def drain():
            copy.wait_send()

        if when is None:
            start()
            drains.append(drain)
        else:
            pl.when(when)(start)
            drains.append(lambda: pl.when(when)(drain))

    def receive(dst, ssem, rsem, when=None):
        copy = pltpu.make_async_remote_copy(
            src_ref=dst, dst_ref=dst, send_sem=ssem, recv_sem=rsem,
            device_id=at(x, y, z, other), device_id_type=pl.DeviceIdType.MESH,
        )
        if when is None:
            copy.wait_recv()
        else:
            pl.when(when)(copy.wait_recv)

    load = pltpu.make_async_copy(e_hbm, e_ref, load_sem)
    load.start()

    barrier = pltpu.get_barrier_semaphore()

    def greet_plane(i, _):
        (x_, y_), _b = xy(i // C)
        pl.semaphore_signal(
            barrier, inc=1, device_id=at(x_, y_, z, (c + i % C) % C),
            device_id_type=pl.DeviceIdType.MESH,
        )
        return 0

    def greet_line(i, _):
        pl.semaphore_signal(
            barrier, inc=1, device_id=at(x, y, (z + i // C) % Z, (c + i % C) % C),
            device_id_type=pl.DeviceIdType.MESH,
        )
        return 0

    lax.fori_loop(1, XY * C, greet_plane, 0)
    lax.fori_loop(C, Z * C, greet_line, 0)
    pl.semaphore_wait(barrier, XY * C - 1 + Z * C - C)

    def gather(piece, full, z_s, z_r, x_s, x_r, c_s, c_r):
        @pl.when(owner)
        def _():
            full[x, c, zl, y] = piece()

        for k in range(1, Z):
            mine = full.at[x, c, zl, y]
            send(mine, mine, z_s.at[k], z_r.at[zl], at(x, y, (z + k) % Z, c), owner)
        for k in range(ZL):
            low = (zl + k) % ZL
            receive(
                full.at[x, c, low, y], z_s.at[0], z_r.at[low],
                jnp.logical_not(owner) if k == 0 else None,
            )
        mine = full.at[x, c, :, y]
        for k in range(1, XY):
            (x_, y_), _b = xy(k)
            send(mine, mine, x_s.at[k], x_r.at[k], at(x_, y_, z, c))
        send(mine, mine, c_s.at[0], c_r.at[0], at(x, y, z, other))
        for k in range(1, XY):
            _f, (x_, y_) = xy(k)
            got = full.at[x_, c, :, y_]
            receive(got, x_s.at[k], x_r.at[k])
            send(got, got, c_s.at[k], c_r.at[k], at(x, y, z, other))
        for k in range(XY):
            _f, (x_, y_) = xy(k)
            receive(full.at[x_, other, :, y_], c_s.at[k], c_r.at[k])

    def times_full(full):
        def step(i, total):
            columns = pl.ds(pl.multiple_of(i * CHUNK, CHUNK), CHUNK)
            block = full[i // C, i % C].reshape(CHUNK, full.shape[-1])
            return total + nn(e_ref[:, columns], block)

        return lax.fori_loop(
            0, X * C, step, jnp.zeros((e_ref.shape[0], full.shape[-1]), F32)
        )

    def scatter_first(left, part, core, summed, landing, c_s, c_r, x_s, x_r):
        def product(kx, half_, slot):
            start = pl.multiple_of(((x + kx) % X) * (C * CHUNK) + half_ * CHUNK, CHUNK)
            block = nn(left, e_ref[:, pl.ds(start, CHUNK)])
            k = left.shape[0]
            block = jnp.concatenate(
                [block[:, i : i + k].T for i in range(0, CHUNK, k)], axis=0
            ).astype(BF16)
            block = block.reshape(ZL, Y, PIECE, k)
            for y_ in range(Y):
                part[kx, slot, y_] = block[:, y_]

        order = (1, 2, 3, 0)
        for kx in order:
            product(kx, other, 0)
            send(part.at[kx, 0], core.at[kx], c_s.at[kx], c_r.at[kx], at(x, y, z, other))
            product(kx, c, 1)
        for kx in order:
            receive(core.at[kx], c_s.at[kx], c_r.at[kx])
            summed[kx] = (part[kx, 1].astype(F32) + core[kx].astype(F32)).astype(BF16)
            for ky in (1, 2, 3, 0):
                k = kx * Y + ky
                if k:
                    (x_, y_), _b = xy(k)
                    send(
                        summed.at[kx, y_], landing.at[k], x_s.at[k], x_r.at[k], at(x_, y_, z, c)
                    )

    def scatter_second(summed, landing, x_s, x_r, zout, zland, z_s, z_r):
        total = summed[0, y].astype(F32)
        for k in range(1, XY):
            receive(landing.at[k], x_s.at[k], x_r.at[k])
            total = total + landing[k].astype(F32)
        zout[...] = total.astype(BF16)
        for k in range(ZL):
            low = (zl + k) % ZL
            send(
                zout.at[low], zland.at[z], z_s.at[k], z_r.at[z], at(x, y, c * ZL + low, c),
                jnp.logical_not(owner) if k == 0 else None,
            )

    def scatter_third(zout, zland, z_s, z_r):
        zland[z] = zout[zl]
        total = None
        for k in range(1, Z):
            from_ = (z + k) % Z
            receive(zland.at[from_], z_s.at[0], z_r.at[from_])
        for k in range(Z):
            term = zland[k].astype(F32)
            total = term if total is None else total + term
        return total

    gather(
        lambda: s_ref[pl.ds(pl.multiple_of(y * PIECE, PIECE), PIECE), :],
        s_full, ags_z_s, ags_z_r, ags_x_s, ags_x_r, ags_c_s, ags_c_r,
    )
    load.wait()
    sketched = times_full(s_full).T.astype(BF16)

    scatter_first(sketched, part_a, core_a, sum_a, xy_a, rsa_c_s, rsa_c_r, rsa_x_s, rsa_x_r)
    scatter_second(sum_a, xy_a, rsa_x_s, rsa_x_r, zout_a, z_a, rsa_z_s, rsa_z_r)
    gather(
        lambda: (scatter_third(zout_a, z_a, rsa_z_s, rsa_z_r) / rows_all).astype(BF16),
        p_full, agp_z_s, agp_z_r, agp_x_s, agp_x_r, agp_c_s, agp_c_r,
    )

    refined = times_full(p_full)
    refined_t = refined.T
    gram = nn(refined_t, refined, HIGHEST) / rows_all
    gpart[...] = gram.reshape(gpart.shape)

    for k in range(XY):
        (x_, y_), _b = xy(k)
        when = jnp.logical_not(owner) if k == 0 else None
        send(
            gpart.at[x_ * Y + y_], g1.at[C * k + c], g1_s.at[k], g1_r.at[C * k + c],
            at(x_, y_, z, half), when,
        )

    scatter_first(
        refined_t.astype(BF16), part_b, core_b, sum_b, xy_b, rsb_c_s, rsb_c_r, rsb_x_s, rsb_x_r
    )

    @pl.when(owner)
    def _():
        g1[c] = gpart[x * Y + y]
        for k in range(1, XY):
            for c_ in range(C):
                receive(g1.at[C * k + c_], g1_s.at[0], g1_r.at[C * k + c_])
        receive(g1.at[other], g1_s.at[0], g1_r.at[other])
        g2[z] = jnp.sum(g1[...], axis=0)

    for k in range(1, Z):
        z_ = (z + k) % Z
        send(g2.at[z], g2.at[z], g2_s.at[k], g2_r.at[z], at(x, y, z_, z_ // ZL), owner)

    @pl.when(owner)
    def _():
        for k in range(1, Z):
            from_ = (z + k) % Z
            receive(g2.at[from_], g2_s.at[0], g2_r.at[from_])
        gfull[x * Y + y] = jnp.sum(g2[...], axis=0)

    for i in range(1, XY * C):
        (x_, y_), _b = xy(i // C)
        mine = gfull.at[x * Y + y]
        send(
            mine, mine, g3_s.at[i], g3_r.at[i // C], at(x_, y_, z, (c + i % C) % C), owner
        )

    scatter_second(sum_b, xy_b, rsb_x_s, rsb_x_r, zout_b, z_b, rsb_z_s, rsb_z_r)
    for k in range(XY):
        _f, (x_, y_) = xy(k)
        receive(
            gfull.at[x_ * Y + y_], g3_s.at[0], g3_r.at[k],
            jnp.logical_not(owner) if k == 0 else None,
        )

    steps = inverse_factor_steps(gfull[...].reshape(gram.shape))
    for i, inverse in enumerate(steps):
        if i == 4:

            @pl.when(owner)
            def _():
                yfin[y] = scatter_third(zout_b, z_b, rsb_z_s, rsb_z_r)

            for j in range(1, Y * C):
                y_, c_ = (y + j // C) % Y, (c + j % C) % C
                send(yfin.at[y], yfin.at[y], f_s.at[j], f_r.at[y], at(x, y_, z, c_), owner)

    ortho_ref[...] = nt(refined, inverse, HIGHEST)
    for k in range(Y):
        from_ = (y + k) % Y
        receive(
            yfin.at[from_], f_s.at[0], f_r.at[from_], jnp.logical_not(owner) if k == 0 else None
        )
    scale = e_ref.shape[1] ** 0.5 / rows_all
    proj_ref[...] = nt(yfin[...].reshape(proj_ref.shape), inverse, HIGHEST) * scale

    for drain in drains:
        drain()


def body(embeddings, sketch_matrix):
    rows, width = embeddings.shape
    k = sketch_matrix.shape[1]
    dma = pltpu.SemaphoreType.DMA
    full = pltpu.VMEM((X, C, ZL, Y, PIECE, k), BF16)
    part = pltpu.VMEM((X, C, Y, ZL, PIECE, k), BF16)
    core = pltpu.VMEM((X, Y, ZL, PIECE, k), BF16)
    landing = pltpu.VMEM((XY, ZL, PIECE, k), BF16)
    zout = pltpu.VMEM((ZL, PIECE, k), BF16)
    zland = pltpu.VMEM((Z, PIECE, k), BF16)
    gather_sems = [dma((Z,)), dma((ZL,)), dma((XY,)), dma((XY,)), dma((XY,)), dma((XY,))]
    scatter_sems = [dma((X,)), dma((X,)), dma((XY,)), dma((XY,)), dma((ZL,)), dma((Z,))]
    return pl.pallas_call(
        kernel,
        out_shape=(
            jax.ShapeDtypeStruct((rows, k), F32),
            jax.ShapeDtypeStruct(sketch_matrix.shape, F32),
        ),
        in_specs=[pl.BlockSpec(memory_space=pl.ANY), pl.BlockSpec(memory_space=pltpu.VMEM)],
        out_specs=[pl.BlockSpec(memory_space=pltpu.VMEM)] * 2,
        scratch_shapes=[
            pltpu.VMEM((rows, width), BF16),
            full, full, part, part, core, core, core, core, landing, landing,
            zout, zout, zland, zland,
            pltpu.VMEM((XY, k // XY, k), F32),
            pltpu.VMEM((XY * C, k // XY, k), F32),
            pltpu.VMEM((Z, k // XY, k), F32),
            pltpu.VMEM((XY, k // XY, k), F32),
            pltpu.VMEM((Y, PIECE, k), F32),
            dma,
            *gather_sems, *gather_sems, *scatter_sems, *scatter_sems,
            dma((XY,)), dma((XY * C,)), dma((Z,)), dma((Z,)), dma((XY * C,)), dma((XY,)),
            dma((Y * C,)), dma((Y,)),
        ],
        compiler_params=pltpu.CompilerParams(
            collective_id=0, has_side_effects=True, vmem_limit_bytes=40 * 1024 * 1024
        ),
        cost_estimate=pl.CostEstimate(
            flops=8 * rows * width * k, bytes_accessed=2 * rows * width, transcendentals=0
        ),
    )(embeddings, sketch_matrix)


def solution(mesh):
    in_specs = (P(("grp", "dev"), None), P("dev", None))
    out_specs = (P(("grp", "dev"), None), P("dev", None))
    return jax.shard_map(body, mesh=mesh, in_specs=in_specs, out_specs=out_specs, check_vma=False)
```

```python
import jax
import jax.numpy as jnp
from jax import lax
from jax.experimental import pallas as pl
from jax.experimental.pallas import tpu as pltpu
from jax.sharding import PartitionSpec as P

X, Y, Z, C = 4, 4, 16, 2
XY = X * Y
ZL = Z // C
DEVICES = XY * Z * C
PIECE = 16
CHUNK = ZL * Y * PIECE
PANEL = 16
BLOCKS = 2
HIGHEST = lax.Precision.HIGHEST
F32, BF16 = jnp.float32, jnp.bfloat16


def far_first(steps, *sizes):
    def hops(k):
        total = 0
        for size in reversed(sizes):
            total += min(k % size, size - k % size)
            k //= size
        return total

    return sorted(steps, key=lambda k: -hops(k))


PLANE = far_first(range(1, XY), X, Y)
LINE = far_first(range(1, Z), Z)
RING = far_first(range(X), X)


def nt(a, b, precision=None):
    return lax.dot_general(
        a, b, (((1,), (1,)), ((), ())), precision=precision, preferred_element_type=F32
    )


def tn(a, b, precision=None):
    return lax.dot_general(
        a, b, (((0,), (0,)), ((), ())), precision=precision, preferred_element_type=F32
    )


def nn(a, b, precision=None):
    return jnp.dot(a, b, precision=precision, preferred_element_type=F32)


def inverse_factor(gram):
    k = gram.shape[0]
    rows = lax.broadcasted_iota(jnp.int32, (PANEL, 1), 0)
    eye = (
        lax.broadcasted_iota(jnp.int32, (k, k), 0) == lax.broadcasted_iota(jnp.int32, (k, k), 1)
    ).astype(F32)
    trailing = jnp.concatenate([gram, eye], axis=1)
    done = []
    for base in range(0, k, PANEL):
        panel = trailing[:PANEL]
        cols = [
            jnp.broadcast_to(panel[:, base + t : base + t + 1], (PANEL, k)) for t in range(PANEL)
        ]
        left, right = panel[:, :k], panel[:, k:]
        for j in range(PANEL):
            pivot = lax.rsqrt(cols[j][j : j + 1])
            factor = cols[j] * pivot
            below = jnp.where(rows > j, factor, 0.0)
            for t in range(j + 1, PANEL):
                cols[t] = cols[t] - below * factor[t : t + 1]
            scale = jnp.where(rows == j, pivot, 1.0)
            left_row, right_row = left[j : j + 1] * pivot, right[j : j + 1] * pivot
            left = left * scale - below * left_row
            right = right * scale - below * right_row
        done.append(right)
        if base + PANEL < k:
            both = jnp.concatenate([left, right], axis=1)
            trailing = trailing[PANEL:] - tn(left[:, base + PANEL :], both, HIGHEST)
    return jnp.concatenate(done, axis=0)


def kernel(
    e_hbm, s_hbm, ortho_ref, proj_ref,
    e_chip, s_piece, s_half, p_half, mine_a, mine_b, theirs_a, theirs_b, right_a, right_b, refined,
    sum_a, sum_b, xy_a, xy_b, zout_a, zout_b, z_a, z_b, gpart, g1, g2, gfull, y_all,
    load_sem, piece_sem, e_s, e_r,
    ags_z_s, ags_z_r, ags_x_s, ags_x_r, ags_c_s, ags_c_r,
    agp_z_s, agp_z_r, agp_x_s, agp_x_r, agp_c_s, agp_c_r,
    rsa_x_s, rsa_x_r, rsa_z_s, rsa_z_r,
    rsb_x_s, rsb_x_r, rsb_z_s, rsb_z_r,
    g1_s, g1_r, g2_s, g2_r, g3_s, g3_r, f_s, f_r,
):
    grp, dev = lax.axis_index("grp"), lax.axis_index("dev")
    y, c = grp // C, grp % C
    x, z = dev // Z, dev % Z
    other = 1 - c
    half, zl = z // ZL, z % ZL
    owner = c == half
    rows, width = e_hbm.shape
    k_all = s_hbm.shape[1]
    rows_all = DEVICES * rows

    def at(x_, y_, z_, c_):
        return (y_ * C + c_, x_ * Z + z_)

    def xy(k):
        kx, ky = k // Y, k % Y
        return ((x + kx) % X, (y + ky) % Y), ((x + X - kx) % X, (y + Y - ky) % Y)

    drains, earlier = [], []

    def drain_earlier():
        for drain in earlier:
            drain()
        earlier[:] = drains
        drains.clear()

    def send(src, dst, ssem, rsem, to, when=None):
        copy = pltpu.make_async_remote_copy(
            src_ref=src, dst_ref=dst, send_sem=ssem, recv_sem=rsem,
            device_id=to, device_id_type=pl.DeviceIdType.MESH,
        )

        def start():
            copy.start()

        def drain():
            copy.wait_send()

        if when is None:
            start()
            drains.append(drain)
        else:
            pl.when(when)(start)
            drains.append(lambda: pl.when(when)(drain))

    def receive(dst, ssem, rsem, when=None):
        copy = pltpu.make_async_remote_copy(
            src_ref=dst, dst_ref=dst, send_sem=ssem, recv_sem=rsem,
            device_id=at(x, y, z, other), device_id_type=pl.DeviceIdType.MESH,
        )
        if when is None:
            copy.wait_recv()
        else:
            pl.when(when)(copy.wait_recv)

    def columns(x_, half_):
        return e_hbm.at[:, pl.ds(pl.multiple_of((x_ * C + half_) * CHUNK, CHUNK), CHUNK)]

    def load(x_):
        return pltpu.make_async_copy(columns(x_, c), e_chip.at[x_, pl.ds(0, rows)], load_sem.at[x_])

    for x_ in range(X):
        load(x_).start()
    load_piece = pltpu.make_async_copy(
        s_hbm.at[pl.ds(pl.multiple_of(y * PIECE, PIECE), PIECE)], s_piece, piece_sem
    )
    load_piece.start()

    barrier = pltpu.get_barrier_semaphore()

    def greet(to):
        pl.semaphore_signal(barrier, inc=1, device_id=to, device_id_type=pl.DeviceIdType.MESH)

    for k in LINE:
        greet(at(x, y, (z + k) % Z, c))
    for k in PLANE:
        (x_, y_), _b = xy(k)
        for c_ in range(C):
            greet(at(x_, y_, z, c_))
    greet(at(x, y, z, other))

    load_piece.wait()
    for x_ in range(X):
        load(x_).wait()
    pl.semaphore_wait(barrier, XY * C - 1 + Z - 1)

    def exchange_embeddings():
        for x_ in range(X):
            send(
                columns(x_, other), e_chip.at[x_, pl.ds(rows, rows)],
                e_s.at[x_], e_r.at[x_], at(x, y, z, other),
            )
        for x_ in range(X):
            receive(e_chip.at[x_, pl.ds(rows, rows)], e_s.at[x_], e_r.at[x_])

    def gather_times(piece, meanwhile, use, full, mine_ref, theirs, z_s, z_r, x_s, x_r, c_s, c_r):
        @pl.when(owner)
        def _():
            full[x, y, zl] = piece()

        for k in LINE:
            mine = full.at[x, y, zl]
            send(mine, mine, z_s.at[k], z_r.at[zl], at(x, y, (z + k) % Z, c), owner)
        drain_earlier()
        meanwhile()
        for k in range(ZL):
            low = (zl + k) % ZL
            receive(
                full.at[x, y, low], z_s.at[0], z_r.at[low],
                jnp.logical_not(owner) if k == 0 else None,
            )
        mine = full.at[x, y]
        for k in PLANE:
            (x_, y_), _b = xy(k)
            send(mine, mine, x_s.at[k], x_r.at[k], at(x_, y_, z, c))
        drain_earlier()

        depth = C * rows // BLOCKS
        for kx in reversed(RING):
            for ky in reversed(RING):
                k = kx * Y + ky
                if k:
                    _f, (x_, y_) = xy(k)
                    receive(full.at[x_, y_], x_s.at[k], x_r.at[k])
            x_ = (x + X - kx) % X
            block = full[x_]
            block = jnp.concatenate(
                [block[y_, low] for low in range(ZL) for y_ in range(Y)], axis=0
            )
            for b in range(BLOCKS):
                here = pl.ds(b * depth, depth)
                term = nn(e_chip[x_, here], block)
                mine_ref[here] = term if kx == 0 else mine_ref[here] + term
                if kx == RING[0]:
                    send(
                        mine_ref.at[here], theirs.at[here], c_s.at[b], c_r.at[b],
                        at(x, y, z, other),
                    )
        for b in range(BLOCKS):
            there = pl.ds(b * depth, depth)
            here = pl.ds((b + BLOCKS // C) % BLOCKS * depth, depth)
            receive(theirs.at[there], c_s.at[b], c_r.at[b])
            use(here, mine_ref[here] + theirs[there])

    def scatter_first(right, summed, landing, x_s, x_r):
        for kx in RING:
            block = tn(e_chip[(x + kx) % X], right[...]).astype(BF16)
            block = block.reshape(ZL, Y, PIECE, right.shape[1])
            for y_ in range(Y):
                summed[kx, y_] = block[:, y_]
            for ky in RING:
                k = kx * Y + ky
                if k:
                    (x_, y_), _b = xy(k)
                    send(
                        summed.at[kx, y_], landing.at[k], x_s.at[k], x_r.at[k], at(x_, y_, z, c)
                    )
        drain_earlier()

    def scatter_second(summed, landing, x_s, x_r, zout, zland, z_s, z_r):
        total = summed[0, y].astype(F32)
        for k in reversed(PLANE):
            receive(landing.at[k], x_s.at[k], x_r.at[k])
            total = total + landing[k].astype(F32)
        zout[...] = total.astype(BF16)
        apart = (c - half) * (c - half)
        for i in range(ZL):
            near, far = ((j + 1) // 2 * (1 if j % 2 else ZL - 1) % ZL for j in (ZL - 1 - i, i))
            low = (zl + near + apart * (far - near + ZL)) % ZL
            send(
                zout.at[low], zland.at[z], z_s.at[i], z_r.at[z], at(x, y, c * ZL + low, c),
                jnp.logical_not(owner) if i == ZL - 1 else None,
            )
        drain_earlier()

    def scatter_third(zout, zland, z_s, z_r):
        zland[z] = zout[zl]
        total = None
        for k in reversed(LINE):
            from_ = (z + k) % Z
            receive(zland.at[from_], z_s.at[0], z_r.at[from_])
        for k in range(Z):
            term = zland[k].astype(F32)
            total = term if total is None else total + term
        return total

    def keep_sketched(here, block):
        right_a[here] = block.astype(BF16)

    gather_times(
        lambda: s_piece[...], exchange_embeddings, keep_sketched,
        s_half, mine_a, theirs_a, ags_z_s, ags_z_r, ags_x_s, ags_x_r, ags_c_s, ags_c_r,
    )

    scatter_first(right_a, sum_a, xy_a, rsa_x_s, rsa_x_r)
    scatter_second(sum_a, xy_a, rsa_x_s, rsa_x_r, zout_a, z_a, rsa_z_s, rsa_z_r)

    def keep_refined(here, block):
        right_b[here] = block.astype(BF16)
        refined[here] = block

    gather_times(
        lambda: (scatter_third(zout_a, z_a, rsa_z_s, rsa_z_r) / rows_all).astype(BF16),
        lambda: None, keep_refined,
        p_half, mine_b, theirs_b, agp_z_s, agp_z_r, agp_x_s, agp_x_r, agp_c_s, agp_c_r,
    )

    gram = tn(refined[...], refined[...], HIGHEST) / rows_all
    gpart[...] = gram.reshape(gpart.shape)

    keeper = c == (x + y) % C
    for k in PLANE:
        (x_, y_), _b = xy(k)
        odd = (k // Y + k % Y) % C
        send(
            gpart.at[x_ * Y + y_], g1.at[k], g1_s.at[k], g1_r.at[k],
            at(x_, y_, z, c), jnp.logical_not(keeper) if odd else keeper,
        )

    scatter_first(right_b, sum_b, xy_b, rsb_x_s, rsb_x_r)

    @pl.when(keeper)
    def _():
        g1[0] = gpart[x * Y + y]
        for k in reversed(PLANE):
            receive(g1.at[k], g1_s.at[0], g1_r.at[k])
        g2[z] = jnp.sum(g1[...], axis=0)

    for k in LINE:
        send(g2.at[z], g2.at[z], g2_s.at[k], g2_r.at[z], at(x, y, (z + k) % Z, c), keeper)

    scatter_second(sum_b, xy_b, rsb_x_s, rsb_x_r, zout_b, z_b, rsb_z_s, rsb_z_r)

    @pl.when(keeper)
    def _():
        for k in reversed(LINE):
            from_ = (z + k) % Z
            receive(g2.at[from_], g2_s.at[0], g2_r.at[from_])
        gfull[x * Y + y] = jnp.sum(g2[...], axis=0)

    mine = gfull.at[x * Y + y]
    for k in (*PLANE, 0):
        (x_, y_), _b = xy(k)
        for c_ in (other, c) if k else (other,):
            i = C * k + (c_ is c)
            send(mine, mine, g3_s.at[i], g3_r.at[k], at(x_, y_, z, c_), keeper)

    @pl.when(owner)
    def _():
        y_all[y] = scatter_third(zout_b, z_b, rsb_z_s, rsb_z_r)

    for j in far_first(range(1, Y * C), Y, C):
        y_, c_ = (y + j // C) % Y, (c + j % C) % C
        send(y_all.at[y], y_all.at[y], f_s.at[j], f_r.at[y], at(x, y_, z, c_), owner)
    drain_earlier()
    drain_earlier()
    for k in (0, *reversed(PLANE)):
        _f, (x_, y_) = xy(k)
        receive(
            gfull.at[x_ * Y + y_], g3_s.at[0], g3_r.at[k], None if k else jnp.logical_not(keeper)
        )

    inverse = inverse_factor(gfull[...].reshape(k_all, k_all))

    ortho_ref[...] = nt(refined[pl.ds(0, rows)], inverse, HIGHEST)
    for k in (0, 3, 1, 2):
        from_ = (y + k) % Y
        receive(
            y_all.at[from_], f_s.at[0], f_r.at[from_], None if k else jnp.logical_not(owner)
        )
    proj_ref[...] = nt(y_all[...].reshape(proj_ref.shape), inverse, HIGHEST) * (
        width**0.5 / rows_all
    )

    drain_earlier()
    drain_earlier()


def body(embeddings, sketch_matrix):
    rows, width = embeddings.shape
    k = sketch_matrix.shape[1]
    dma = pltpu.SemaphoreType.DMA
    half = pltpu.VMEM((X, Y, ZL, PIECE, k), BF16)
    partial = pltpu.VMEM((C * rows, k), F32)
    right = pltpu.VMEM((C * rows, k), BF16)
    landing = pltpu.VMEM((XY, ZL, PIECE, k), BF16)
    zout = pltpu.VMEM((ZL, PIECE, k), BF16)
    zland = pltpu.VMEM((Z, PIECE, k), BF16)
    gather_sems = [dma((Z,)), dma((ZL,)), dma((XY,)), dma((XY,))]
    gather_sems += [dma((BLOCKS,)), dma((BLOCKS,))]
    scatter_sems = [dma((XY,)), dma((XY,)), dma((ZL,)), dma((Z,))]
    return pl.pallas_call(
        kernel,
        out_shape=(
            jax.ShapeDtypeStruct((rows, k), F32),
            jax.ShapeDtypeStruct(sketch_matrix.shape, F32),
        ),
        in_specs=[pl.BlockSpec(memory_space=pltpu.HBM)] * 2,
        out_specs=[pl.BlockSpec(memory_space=pltpu.VMEM)] * 2,
        scratch_shapes=[
            pltpu.VMEM((X, C * rows, CHUNK), BF16),
            pltpu.VMEM((PIECE, k), BF16),
            half, half, partial, partial, partial, partial, right, right, partial, half, half, landing, landing,
            zout, zout, zland, zland,
            pltpu.VMEM((XY, k // XY, k), F32),
            pltpu.VMEM((XY, k // XY, k), F32),
            pltpu.VMEM((Z, k // XY, k), F32),
            pltpu.VMEM((XY, k // XY, k), F32),
            pltpu.VMEM((Y, PIECE, k), F32),
            dma((X,)), dma, dma((X,)), dma((X,)),
            *gather_sems, *gather_sems, *scatter_sems, *scatter_sems,
            dma((XY,)), dma((XY,)), dma((Z,)), dma((Z,)), dma((XY * C,)), dma((XY,)),
            dma((Y * C,)), dma((Y,)),
        ],
        compiler_params=pltpu.CompilerParams(
            collective_id=0, has_side_effects=True, vmem_limit_bytes=52 * 1024 * 1024
        ),
        cost_estimate=pl.CostEstimate(
            flops=8 * rows * width * k, bytes_accessed=2 * rows * width, transcendentals=0
        ),
    )(embeddings, sketch_matrix)


def solution(mesh):
    in_specs = (P(("grp", "dev"), None), P("dev", None))
    out_specs = (P(("grp", "dev"), None), P("dev", None))
    return jax.shard_map(body, mesh=mesh, in_specs=in_specs, out_specs=out_specs, check_vma=False)
```

```python
import jax
import jax.numpy as jnp
from jax import lax
from jax.experimental import pallas as pl
from jax.experimental.pallas import tpu as pltpu
from jax.sharding import PartitionSpec as P

X, Y, Z, C = 4, 4, 16, 2
XY = X * Y
ZL = Z // C
DEVICES = XY * Z * C
PIECE = 16
CHUNK = ZL * Y * PIECE
PANEL = 32
BLOCKS = 2
HIGHEST = lax.Precision.HIGHEST
F32, BF16 = jnp.float32, jnp.bfloat16


def far_first(steps, *sizes):
    def hops(k):
        total = 0
        for size in reversed(sizes):
            total += min(k % size, size - k % size)
            k //= size
        return total

    return sorted(steps, key=lambda k: -hops(k))


PLANE = far_first(range(1, XY), X, Y)
LINE = far_first(range(1, Z), Z)
RING = far_first(range(X), X)


def nt(a, b, precision=None):
    return lax.dot_general(
        a, b, (((1,), (1,)), ((), ())), precision=precision, preferred_element_type=F32
    )


def tn(a, b, precision=None):
    return lax.dot_general(
        a, b, (((0,), (0,)), ((), ())), precision=precision, preferred_element_type=F32
    )


def nn(a, b, precision=None):
    return jnp.dot(a, b, precision=precision, preferred_element_type=F32)


def inverse_factor(gram):
    k = gram.shape[0]
    rows = lax.broadcasted_iota(jnp.int32, (PANEL, 1), 0)
    eye = (
        lax.broadcasted_iota(jnp.int32, (k, k), 0) == lax.broadcasted_iota(jnp.int32, (k, k), 1)
    ).astype(F32)
    trailing = jnp.concatenate([gram, eye], axis=1)
    done = []
    for base in range(0, k, PANEL):
        panel = trailing[:PANEL]
        cols = [
            jnp.broadcast_to(panel[:, base + t : base + t + 1], (PANEL, k)) for t in range(PANEL)
        ]
        left, right = panel[:, :k], panel[:, k:]
        for j in range(PANEL):
            pivot = lax.rsqrt(cols[j][j : j + 1])
            factor = cols[j] * pivot
            below = jnp.where(rows > j, factor, 0.0)
            for t in range(j + 1, PANEL):
                cols[t] = cols[t] - below * factor[t : t + 1]
            scale = jnp.where(rows == j, pivot, 1.0)
            left_row, right_row = left[j : j + 1] * pivot, right[j : j + 1] * pivot
            left = left * scale - below * left_row
            right = right * scale - below * right_row
        done.append(right)
        if base + PANEL < k:
            both = jnp.concatenate([left, right], axis=1)
            trailing = trailing[PANEL:] - tn(left[:, base + PANEL :], both, HIGHEST)
    return jnp.concatenate(done, axis=0)


def kernel(
    e_hbm, s_hbm, ortho_ref, proj_ref,
    e_chip, s_piece, s_half, p_half, mine_a, mine_b, theirs_a, theirs_b, right_a, right_b, refined,
    sum_a, sum_b, xy_a, xy_b, zout_a, zout_b, z_a, z_b, gpart, g1, g2, gfull, y_all,
    load_sem, piece_sem, e_s, e_r,
    ags_z_s, ags_z_r, ags_x_s, ags_x_r, ags_c_s, ags_c_r,
    agp_z_s, agp_z_r, agp_x_s, agp_x_r, agp_c_s, agp_c_r,
    rsa_x_s, rsa_x_r, rsa_z_s, rsa_z_r,
    rsb_x_s, rsb_x_r, rsb_z_s, rsb_z_r,
    g1_s, g1_r, g2_s, g2_r, g3_s, g3_r, f_s, f_r,
):
    grp, dev = lax.axis_index("grp"), lax.axis_index("dev")
    y, c = grp // C, grp % C
    x, z = dev // Z, dev % Z
    other = 1 - c
    half, zl = z // ZL, z % ZL
    owner = c == half
    rows, width = e_hbm.shape
    k_all = s_hbm.shape[1]
    rows_all = DEVICES * rows

    def at(x_, y_, z_, c_):
        return (y_ * C + c_, x_ * Z + z_)

    def xy(k):
        kx, ky = k // Y, k % Y
        return ((x + kx) % X, (y + ky) % Y), ((x + X - kx) % X, (y + Y - ky) % Y)

    drains, earlier = [], []

    def drain_earlier():
        for drain in earlier:
            drain()
        earlier[:] = drains
        drains.clear()

    def send(src, dst, ssem, rsem, to, when=None):
        copy = pltpu.make_async_remote_copy(
            src_ref=src, dst_ref=dst, send_sem=ssem, recv_sem=rsem,
            device_id=to, device_id_type=pl.DeviceIdType.MESH,
        )

        def start():
            copy.start()

        def drain():
            copy.wait_send()

        if when is None:
            start()
            drains.append(drain)
        else:
            pl.when(when)(start)
            drains.append(lambda: pl.when(when)(drain))

    def receive(dst, ssem, rsem, when=None):
        copy = pltpu.make_async_remote_copy(
            src_ref=dst, dst_ref=dst, send_sem=ssem, recv_sem=rsem,
            device_id=at(x, y, z, other), device_id_type=pl.DeviceIdType.MESH,
        )
        if when is None:
            copy.wait_recv()
        else:
            pl.when(when)(copy.wait_recv)

    def columns(x_, half_):
        return e_hbm.at[:, pl.ds(pl.multiple_of((x_ * C + half_) * CHUNK, CHUNK), CHUNK)]

    def load(x_):
        return pltpu.make_async_copy(columns(x_, c), e_chip.at[x_, pl.ds(0, rows)], load_sem.at[x_])

    for x_ in range(X):
        load(x_).start()
    load_piece = pltpu.make_async_copy(
        s_hbm.at[pl.ds(pl.multiple_of(y * PIECE, PIECE), PIECE)], s_piece, piece_sem
    )
    load_piece.start()

    barrier = pltpu.get_barrier_semaphore()

    def greet(to):
        pl.semaphore_signal(barrier, inc=1, device_id=to, device_id_type=pl.DeviceIdType.MESH)

    for k in LINE:
        greet(at(x, y, (z + k) % Z, c))
    for k in PLANE:
        (x_, y_), _b = xy(k)
        for c_ in range(C):
            greet(at(x_, y_, z, c_))
    greet(at(x, y, z, other))

    load_piece.wait()
    for x_ in range(X):
        load(x_).wait()
    pl.semaphore_wait(barrier, XY * C - 1 + Z - 1)

    def exchange_embeddings():
        for x_ in range(X):
            send(
                columns(x_, other), e_chip.at[x_, pl.ds(rows, rows)],
                e_s.at[x_], e_r.at[x_], at(x, y, z, other),
            )
        for x_ in range(X):
            receive(e_chip.at[x_, pl.ds(rows, rows)], e_s.at[x_], e_r.at[x_])

    def gather_times(piece, meanwhile, use, full, mine_ref, theirs, z_s, z_r, x_s, x_r, c_s, c_r):
        @pl.when(owner)
        def _():
            full[x, y, zl] = piece()

        for k in LINE:
            mine = full.at[x, y, zl]
            send(mine, mine, z_s.at[k], z_r.at[zl], at(x, y, (z + k) % Z, c), owner)
        drain_earlier()
        meanwhile()
        for k in range(ZL):
            low = (zl + k) % ZL
            receive(
                full.at[x, y, low], z_s.at[0], z_r.at[low],
                jnp.logical_not(owner) if k == 0 else None,
            )
        mine = full.at[x, y]
        for k in PLANE:
            (x_, y_), _b = xy(k)
            send(mine, mine, x_s.at[k], x_r.at[k], at(x_, y_, z, c))
        drain_earlier()

        depth = C * rows // BLOCKS
        for kx in reversed(RING):
            for ky in reversed(RING):
                k = kx * Y + ky
                if k:
                    _f, (x_, y_) = xy(k)
                    receive(full.at[x_, y_], x_s.at[k], x_r.at[k])
            x_ = (x + X - kx) % X
            block = full[x_]
            block = jnp.concatenate(
                [block[y_, low] for low in range(ZL) for y_ in range(Y)], axis=0
            )
            for b in range(BLOCKS):
                here = pl.ds(b * depth, depth)
                term = nn(e_chip[x_, here], block)
                mine_ref[here] = term if kx == 0 else mine_ref[here] + term
                if kx == RING[0]:
                    send(
                        mine_ref.at[here], theirs.at[here], c_s.at[b], c_r.at[b],
                        at(x, y, z, other),
                    )
        for b in range(BLOCKS):
            there = pl.ds(b * depth, depth)
            here = pl.ds((b + BLOCKS // C) % BLOCKS * depth, depth)
            receive(theirs.at[there], c_s.at[b], c_r.at[b])
            use(here, mine_ref[here] + theirs[there])

    def scatter_first(right, summed, landing, x_s, x_r):
        for kx in RING:
            block = tn(e_chip[(x + kx) % X], right[...]).astype(BF16)
            block = block.reshape(ZL, Y, PIECE, right.shape[1])
            for y_ in range(Y):
                summed[kx, y_] = block[:, y_]
            for ky in RING:
                k = kx * Y + ky
                if k:
                    (x_, y_), _b = xy(k)
                    send(
                        summed.at[kx, y_], landing.at[k], x_s.at[k], x_r.at[k], at(x_, y_, z, c)
                    )
        drain_earlier()

    def scatter_second(summed, landing, x_s, x_r, zout, zland, z_s, z_r):
        total = summed[0, y].astype(F32)
        for k in reversed(PLANE):
            receive(landing.at[k], x_s.at[k], x_r.at[k])
            total = total + landing[k].astype(F32)
        zout[...] = total.astype(BF16)
        apart = (c - half) * (c - half)
        for i in range(ZL):
            near, far = ((j + 1) // 2 * (1 if j % 2 else ZL - 1) % ZL for j in (ZL - 1 - i, i))
            low = (zl + near + apart * (far - near + ZL)) % ZL
            send(
                zout.at[low], zland.at[z], z_s.at[i], z_r.at[z], at(x, y, c * ZL + low, c),
                jnp.logical_not(owner) if i == ZL - 1 else None,
            )
        drain_earlier()

    def scatter_third(zout, zland, z_s, z_r):
        zland[z] = zout[zl]
        total = None
        for k in reversed(LINE):
            from_ = (z + k) % Z
            receive(zland.at[from_], z_s.at[0], z_r.at[from_])
        for k in range(Z):
            term = zland[k].astype(F32)
            total = term if total is None else total + term
        return total

    def keep_sketched(here, block):
        right_a[here] = block.astype(BF16)

    gather_times(
        lambda: s_piece[...], exchange_embeddings, keep_sketched,
        s_half, mine_a, theirs_a, ags_z_s, ags_z_r, ags_x_s, ags_x_r, ags_c_s, ags_c_r,
    )

    scatter_first(right_a, sum_a, xy_a, rsa_x_s, rsa_x_r)
    scatter_second(sum_a, xy_a, rsa_x_s, rsa_x_r, zout_a, z_a, rsa_z_s, rsa_z_r)

    def keep_refined(here, block):
        right_b[here] = block.astype(BF16)
        refined[here] = block

    gather_times(
        lambda: (scatter_third(zout_a, z_a, rsa_z_s, rsa_z_r) / rows_all).astype(BF16),
        lambda: None, keep_refined,
        p_half, mine_b, theirs_b, agp_z_s, agp_z_r, agp_x_s, agp_x_r, agp_c_s, agp_c_r,
    )

    gram = tn(refined[...], refined[...], HIGHEST) / rows_all
    gpart[...] = gram.reshape(gpart.shape)

    keeper = c == (x + y) % C
    for k in PLANE:
        (x_, y_), _b = xy(k)
        odd = (k // Y + k % Y) % C
        send(
            gpart.at[x_ * Y + y_], g1.at[k], g1_s.at[k], g1_r.at[k],
            at(x_, y_, z, c), jnp.logical_not(keeper) if odd else keeper,
        )

    scatter_first(right_b, sum_b, xy_b, rsb_x_s, rsb_x_r)

    @pl.when(keeper)
    def _():
        g1[0] = gpart[x * Y + y]
        for k in reversed(PLANE):
            receive(g1.at[k], g1_s.at[0], g1_r.at[k])
        g2[z] = jnp.sum(g1[...], axis=0)

    for k in LINE:
        send(g2.at[z], g2.at[z], g2_s.at[k], g2_r.at[z], at(x, y, (z + k) % Z, c), keeper)

    scatter_second(sum_b, xy_b, rsb_x_s, rsb_x_r, zout_b, z_b, rsb_z_s, rsb_z_r)

    @pl.when(keeper)
    def _():
        for k in reversed(LINE):
            from_ = (z + k) % Z
            receive(g2.at[from_], g2_s.at[0], g2_r.at[from_])
        gfull[x * Y + y] = jnp.sum(g2[...], axis=0)

    mine = gfull.at[x * Y + y]
    for k in (*PLANE, 0):
        (x_, y_), _b = xy(k)
        for c_ in (other, c) if k else (other,):
            i = C * k + (c_ is c)
            send(mine, mine, g3_s.at[i], g3_r.at[k], at(x_, y_, z, c_), keeper)

    @pl.when(owner)
    def _():
        y_all[y] = scatter_third(zout_b, z_b, rsb_z_s, rsb_z_r)

    for j in far_first(range(1, Y * C), Y, C):
        y_, c_ = (y + j // C) % Y, (c + j % C) % C
        send(y_all.at[y], y_all.at[y], f_s.at[j], f_r.at[y], at(x, y_, z, c_), owner)
    drain_earlier()
    drain_earlier()
    for k in (0, *reversed(PLANE)):
        _f, (x_, y_) = xy(k)
        receive(
            gfull.at[x_ * Y + y_], g3_s.at[0], g3_r.at[k], None if k else jnp.logical_not(keeper)
        )

    inverse = inverse_factor(gfull[...].reshape(k_all, k_all))

    ortho_ref[...] = nt(refined[pl.ds(0, rows)], inverse, HIGHEST)
    for k in (0, 3, 1, 2):
        from_ = (y + k) % Y
        receive(
            y_all.at[from_], f_s.at[0], f_r.at[from_], None if k else jnp.logical_not(owner)
        )
    proj_ref[...] = nt(y_all[...].reshape(proj_ref.shape), inverse, HIGHEST) * (
        width**0.5 / rows_all
    )

    drain_earlier()
    drain_earlier()


def body(embeddings, sketch_matrix):
    rows, width = embeddings.shape
    k = sketch_matrix.shape[1]
    dma = pltpu.SemaphoreType.DMA
    half = pltpu.VMEM((X, Y, ZL, PIECE, k), BF16)
    partial = pltpu.VMEM((C * rows, k), F32)
    right = pltpu.VMEM((C * rows, k), BF16)
    landing = pltpu.VMEM((XY, ZL, PIECE, k), BF16)
    zout = pltpu.VMEM((ZL, PIECE, k), BF16)
    zland = pltpu.VMEM((Z, PIECE, k), BF16)
    gather_sems = [dma((Z,)), dma((ZL,)), dma((XY,)), dma((XY,))]
    gather_sems += [dma((BLOCKS,)), dma((BLOCKS,))]
    scatter_sems = [dma((XY,)), dma((XY,)), dma((ZL,)), dma((Z,))]
    return pl.pallas_call(
        kernel,
        out_shape=(
            jax.ShapeDtypeStruct((rows, k), F32),
            jax.ShapeDtypeStruct(sketch_matrix.shape, F32),
        ),
        in_specs=[pl.BlockSpec(memory_space=pltpu.HBM)] * 2,
        out_specs=[pl.BlockSpec(memory_space=pltpu.VMEM)] * 2,
        scratch_shapes=[
            pltpu.VMEM((X, C * rows, CHUNK), BF16),
            pltpu.VMEM((PIECE, k), BF16),
            half, half, partial, partial, partial, partial, right, right, partial, half, half, landing, landing,
            zout, zout, zland, zland,
            pltpu.VMEM((XY, k // XY, k), F32),
            pltpu.VMEM((XY, k // XY, k), F32),
            pltpu.VMEM((Z, k // XY, k), F32),
            pltpu.VMEM((XY, k // XY, k), F32),
            pltpu.VMEM((Y, PIECE, k), F32),
            dma((X,)), dma, dma((X,)), dma((X,)),
            *gather_sems, *gather_sems, *scatter_sems, *scatter_sems,
            dma((XY,)), dma((XY,)), dma((Z,)), dma((Z,)), dma((XY * C,)), dma((XY,)),
            dma((Y * C,)), dma((Y,)),
        ],
        compiler_params=pltpu.CompilerParams(
            collective_id=0, has_side_effects=True, vmem_limit_bytes=52 * 1024 * 1024
        ),
        cost_estimate=pl.CostEstimate(
            flops=8 * rows * width * k, bytes_accessed=2 * rows * width, transcendentals=0
        ),
    )(embeddings, sketch_matrix)


def solution(mesh):
    in_specs = (P(("grp", "dev"), None), P("dev", None))
    out_specs = (P(("grp", "dev"), None), P("dev", None))
    return jax.shard_map(body, mesh=mesh, in_specs=in_specs, out_specs=out_specs, check_vma=False)
```
